32 devices in a mesh: tok: 4 (over x, core), con: 2 (over y), out: 4 (over z).
Axes of the slice: x: 2, y: 2, z: 4, core: 2. Of those that a mesh axis runs over, the one named last changes fastest.
Arguments:
- tokens: bfloat16 [2048, 10240], P('tok', ('con', 'out')), may hold values from -200 to 200, as said below
- gain: bfloat16 [10240], P(('con', 'out')), may hold values from 0.099609375 to 1.8984375
- up_weight: bfloat16 [10240, 2, 10240], P('con', None, 'out'), may hold values from -0.0625 to 0.0625
- down_weight: bfloat16 [20480, 10240], P(('con', 'out')), may hold values from -0.0625 to 0.0625
Outputs:
- block_out: bfloat16 [2048, 10240], P('tok', ('con', 'out'))
The draws below stay inside these ranges and needn't reach their ends.
Inputs may be any that keep to these rules, and one draw needn't show every extreme that they name: `tokens`: activations of the residual stream.
All inputs are finite; a program needn't handle non-finite values.
Results may differ from the reference program's by a relative error of at most 0.028.
Values may be sent and summed in bfloat16 or wider, within the bound.
No kernel may reach another device: no remote copies, remote signals or barrier semaphores. Data moves between devices by JAX's collectives and lax.ppermute only.
A program may use at most 192 MiB of HBM per device.

```python
import jax
import jax.numpy as jnp
from jax import lax

D = 10240
FFW = 20480
TOKENS = 2048
UNITS = 2560
N_CON = 2
N_OUT = 4


def draw_tokens(key, part):
    first, second, third = jax.random.split(key, 3)
    place = jnp.arange(D, dtype=jnp.float32) / D
    column_scale = jnp.power(10.0, 0.5 * place + 0.5 * jax.random.uniform(second, (D,), jnp.float32))
    base = jnp.clip(jax.random.normal(first, (TOKENS, D), jnp.float32), -5.0, 5.0)
    row_scale = jnp.power(10.0, jax.random.uniform(third, (TOKENS, 1), jnp.float32))
    return (0.3 * base * column_scale * row_scale).astype(jnp.bfloat16)


def raised(values, own_key, source, target, parts, factor):
    owner, partner = [(jnp.arange(values.shape[position]) // (values.shape[position] // parts)).reshape([-1 if axis == position else 1 for axis in range(values.ndim)]) for position in (source, target)]
    chosen = jax.random.permutation(own_key, parts)[partner]
    strong = (owner == chosen) | (owner == (partner + parts // 2) % parts)
    return jnp.where(strong, factor * values, values)


def shard_levels(rng, shape, cuts, least, top_value):
    def one(axis_at, shards_of):
        steps = jax.random.uniform(jax.random.fold_in(jax.random.fold_in(rng, 6), axis_at), (shards_of,), jnp.float32, least / len(cuts), top_value / len(cuts))
        return jnp.repeat(jnp.exp(steps), shape[axis_at] // shards_of).reshape((-1,) + (1,) * (len(shape) - axis_at - 1))

    level = one(*cuts[0])
    for cut in cuts[1:]:
        level = level * one(*cut)
    return level


def bell_draw(own_key, extent, scale, most, pieces=(), held_as=jnp.bfloat16):
    drawn = jax.random.normal(own_key, extent, jnp.float32) * scale
    if len(pieces) > 0:
        drawn = shard_levels(own_key, extent, pieces, -0.22, 0.18) * drawn
    return jnp.clip(drawn, min=-most, max=most).astype(held_as)


def bell_draw_with(key, extent, width, limit, cuts, heavy, kind=jnp.bfloat16):
    result = width * jax.random.normal(key, extent, jnp.float32)
    if cuts:
        result = result * shard_levels(key, extent, cuts, -0.22, 0.18)
    return jnp.clip(raised(result, jax.random.fold_in(key, 3), *heavy), -limit, limit).astype(kind)


def setup_inputs(seed: int = 0) -> dict:
    key_of = jax.random.split(jax.random.key(seed), 5)
    return {
        "tokens": draw_tokens(jax.random.fold_in(key_of[4], 71), 0),
        "gain": jnp.clip(1.0 + 0.18 * jax.random.normal(key_of[1], (D,), jnp.float32), 0.099609375, 1.8984375).astype(jnp.bfloat16),
        "up_weight": bell_draw(key_of[2], (D, N_CON, FFW // N_CON), D ** -0.5, 0.0625, ((0, 2), (2, 4))),
        "down_weight": bell_draw_with(key_of[3], (FFW, D), FFW ** -0.5, 0.0625, ((0, 8),), (0, 1, 8, 2.0)),
    }


def reference(tokens, gain, up_weight, down_weight):
    values = tokens.astype(jnp.float32)
    average = lax.optimization_barrier(jnp.sum(values, axis=1, keepdims=True)) / D
    variance = lax.optimization_barrier(jnp.sum(values * values, axis=1, keepdims=True)) / D - average * average
    normed = ((values - average) * lax.rsqrt(variance + 1e-05) * gain.astype(jnp.float32)).astype(jnp.bfloat16)
    up_matrix = up_weight.reshape(D, FFW)
    preact = jnp.dot(normed, up_matrix, preferred_element_type=jnp.float32)
    hidden = jax.nn.gelu(preact, approximate=False).astype(jnp.bfloat16)
    groups = N_CON * N_OUT

    def add_group(index, total):
        begin = (index * UNITS).astype(jnp.int32)
        hidden_part = lax.dynamic_slice_in_dim(hidden, begin, UNITS, 1)
        weight_part = lax.dynamic_slice_in_dim(down_weight, begin, UNITS, 0)
        term = jnp.dot(hidden_part, weight_part, preferred_element_type=jnp.float32).astype(jnp.bfloat16)
        term = lax.optimization_barrier(term)
        return total + term.astype(jnp.float32)
    start_total = jnp.zeros((TOKENS, D), jnp.float32)
    total = lax.fori_loop(jnp.int32(0), jnp.int32(groups), add_group, start_total)
    return total.astype(jnp.bfloat16)
```

```python
import functools

import jax
import jax.numpy as jnp
from jax import lax
from jax.experimental import pallas as pl
from jax.experimental.pallas import tpu as pltpu
from jax.sharding import PartitionSpec as P

D = 10240
CHUNKS = (7, 9)


def order_of(line):
    return (
        [("norm", 0), ("upo", 0, 0), ("upo", 0, 1), ("upw", 0), ("gelu", 0, 0), ("gelu", 0, 1)]
        + [("s", 0, "o"), ("s", 0, "w"), ("norm", 1), ("upo", 1, 0), ("upo", 1, 1)]
        + [("upw", 1), ("gelu", 1, 0), ("gelu", 1, 1)]
        + [("do", 1, 0, 1), ("do", 1, 1, 1), ("do", 1, 2, line - 2)]
        + [("dw", 1, 0, line // 2), ("m", 1, 0)]
        + [("dw", 1, line // 2, line - line // 2)]
        + [("m", 1, k) for k in range(1, line - 1)]
        + [("x", 0), ("sum", 0), ("fin", 1)]
    )


def tile_of(width):
    return next(tile for tile in (512, 256, 128) if width % tile == 0)


def up_kernel(side_ref, left_ref, right_ref, *refs):
    out_ref = refs[-1]
    out_ref[...] = jnp.dot(
        left_ref[...], right_ref[0], preferred_element_type=jnp.float32
    ).astype(out_ref.dtype)


def up_product(normed, weights, side, first, count, tile, dtype, after):
    rows, depth = normed.shape
    return pl.pallas_call(
        up_kernel,
        grid_spec=pltpu.PrefetchScalarGridSpec(
            num_scalar_prefetch=1,
            grid=(count,),
            in_specs=[
                pl.BlockSpec((rows, depth), lambda j, side: (0, 0)),
                pl.BlockSpec((1, depth, tile), lambda j, side: (side[0], 0, first + j)),
            ]
            + [pl.BlockSpec(memory_space=pl.ANY)] * len(after),
            out_specs=pl.BlockSpec((rows, tile), lambda j, side: (0, j)),
        ),
        out_shape=jax.ShapeDtypeStruct((rows, count * tile), dtype),
        compiler_params=pltpu.CompilerParams(vmem_limit_bytes=40 * 2**20),
        cost_estimate=pl.CostEstimate(flops=1000, bytes_accessed=1000, transcendentals=0),
        name="up_product",
    )(side, normed, weights, *after)


def down_kernel(parts, waits, blocks_ref, *refs):
    lefts, right_ref, outs = refs[:parts], refs[parts], refs[parts + 1 + waits :]
    total, begin = None, 0
    for left in lefts:
        depth = left.shape[1]
        term = jnp.dot(
            left[...], right_ref[begin : begin + depth, :], preferred_element_type=jnp.float32
        )
        total = term if total is None else total + term
        begin += depth
    for k, out in enumerate(outs):

        @pl.when(pl.program_id(0) == k)
        def _(out=out):
            out[...] = total.astype(out.dtype)


def down_products(hidden, weights, table, first, count, columns, after=()):
    rows = hidden[0].shape[0]
    if columns % 128:
        whole = jnp.concatenate(hidden, axis=1)
        return [
            jnp.dot(
                whole,
                lax.dynamic_slice_in_dim(weights, table[first + k] * columns, columns, 1),
                preferred_element_type=jnp.float32,
            ).astype(jnp.bfloat16)
            for k in range(count)
        ]
    return pl.pallas_call(
        functools.partial(down_kernel, len(hidden), len(after)),
        grid_spec=pltpu.PrefetchScalarGridSpec(
            num_scalar_prefetch=1,
            grid=(count,),
            in_specs=[pl.BlockSpec(part.shape, lambda j, table: (0, 0)) for part in hidden]
            + [
                pl.BlockSpec(
                    (weights.shape[0], columns), lambda j, table: (0, table[first + j])
                )
            ]
            + [pl.BlockSpec(memory_space=pl.ANY)] * len(after),
            out_specs=[pl.BlockSpec((rows, columns), lambda j, table: (0, 0))] * count,
        ),
        out_shape=[jax.ShapeDtypeStruct((rows, columns), jnp.bfloat16)] * count,
        compiler_params=pltpu.CompilerParams(vmem_limit_bytes=40 * 2**20),
        cost_estimate=pl.CostEstimate(flops=1000, bytes_accessed=1000, transcendentals=0),
        name="down_products",
    )(table, *hidden, weights, *after)


def stacked_kernel(parts, side_ref, *refs):
    lefts, right_ref, out_ref = refs[:parts], refs[parts], refs[-1]
    total, begin = None, 0
    for left in lefts:
        depth = left.shape[1]
        term = jnp.dot(
            left[...], right_ref[begin : begin + depth, :], preferred_element_type=jnp.float32
        )
        total = term if total is None else total + term
        begin += depth
    out_ref[0] = total.astype(out_ref.dtype)


def stacked_products(hidden, weights, side, line, columns, after):
    rows = hidden[0].shape[0]
    if columns % 128:
        table = side[0] * line + jnp.arange(line, dtype=jnp.int32)
        return jnp.stack(down_products(hidden, weights, table, 0, line, columns))
    return pl.pallas_call(
        functools.partial(stacked_kernel, len(hidden)),
        grid_spec=pltpu.PrefetchScalarGridSpec(
            num_scalar_prefetch=1,
            grid=(line,),
            in_specs=[pl.BlockSpec(piece.shape, lambda p, side: (0, 0)) for piece in hidden]
            + [pl.BlockSpec((weights.shape[0], columns), lambda p, side: (0, side[0] * line + p))]
            + [pl.BlockSpec(memory_space=pl.ANY)] * len(after),
            out_specs=pl.BlockSpec((1, rows, columns), lambda p, side: (p, 0, 0)),
        ),
        out_shape=jax.ShapeDtypeStruct((line, rows, columns), jnp.bfloat16),
        compiler_params=pltpu.CompilerParams(vmem_limit_bytes=40 * 2**20),
        cost_estimate=pl.CostEstimate(flops=1000, bytes_accessed=1000, transcendentals=0),
        name="stacked_products",
    )(side, *hidden, weights, *after)


def normalize(values, totals, gain_row):
    average = totals[0][:, None] / D
    variance = totals[1][:, None] / D - average * average
    return ((values - average) * lax.rsqrt(variance + 1e-05) * gain_row).astype(jnp.bfloat16)


def local(tokens, gain, up_weight, down_weight):
    rows, columns = tokens.shape
    line = lax.axis_size("out")
    half, place = lax.axis_index("con"), lax.axis_index("out")
    swap = [(0, 1), (1, 0)]
    wide = lambda x: x.astype(jnp.float32)

    cuts = [rows * sum(CHUNKS[:i]) // sum(CHUNKS) for i in range(len(CHUNKS) + 1)]
    spans = list(zip(cuts[:-1], cuts[1:]))
    gathered = [lax.all_gather(tokens[a:b], "out", axis=1, tiled=True) for a, b in spans]

    values = wide(tokens)
    mine = jnp.stack([jnp.sum(values, axis=1), jnp.sum(values * values, axis=1)])
    shifts = sorted(range(line), key=lambda s: (-min(s, line - s), s))
    row = (place + jnp.array(shifts, jnp.int32)) % line
    table = jnp.concatenate([(1 - half) * line + row, half * line + row])
    here = half.astype(jnp.int32).reshape(1)
    picks = {"o": 1 - here, "w": here}
    table, picks, mine = lax.optimization_barrier((table, picks, mine))
    mine = mine + lax.ppermute(mine, "con", swap)
    mine = jnp.concatenate([mine.reshape(1, 2 * rows), wide(gain).reshape(1, columns)], axis=1)
    around = [mine] + [
        lax.ppermute(mine, "out", [(p, (p + s) % line) for p in range(line)]) for s in range(1, line)
    ]
    totals = sum(part[0, : 2 * rows] for part in around).reshape(2, rows)
    stacked = jnp.concatenate(around, axis=0)[:, 2 * rows :]
    gain_row = jnp.concatenate(
        [lax.dynamic_index_in_dim(stacked, (place - p + line) % line, 0, False) for p in range(line)]
    )
    totals, gain_row = lax.optimization_barrier((totals, gain_row))

    width = up_weight.shape[2]
    tile = tile_of(width)
    tiles = width // tile
    split = [0, (3 * tiles + 4) // 5, tiles]
    weights = lax.optimization_barrier(jnp.transpose(up_weight, (1, 0, 2)))
    last = [weights]
    have = {}

    def run(f, *args):
        out = f(*args, after=tuple(last))
        last[:] = [out[0] if isinstance(out, (list, tuple)) else out]
        return out

    def plain(f, *args):
        last.append(f(*args))
        return last[-1]

    def task(kind, c, k=0, count=0, *awaited):
        last.extend(have[key] for key in awaited)
        a, b = spans[c]
        if kind == "norm":
            have[kind, c] = plain(
                lambda x, t, g: normalize(wide(x), t, g), gathered[c], totals[:, a:b], gain_row
            )
        elif kind == "upo":
            first, count = split[k], split[k + 1] - split[k]
            out = run(
                lambda x, w, after: up_product(
                    x, w, picks["o"], first, count, tile, jnp.bfloat16, after
                ),
                have["norm", c],
                weights,
            )
            have[kind, c, k] = lax.ppermute(out, "con", swap)
        elif kind == "upw":
            have[kind, c] = run(
                lambda x, w, after: up_product(
                    x, w, picks["w"], 0, tiles, tile, jnp.float32, after
                ),
                have["norm", c],
                weights,
            )
        elif kind == "gelu":
            if k:
                have["gelu", c, 0], have["upo", c, 1] = lax.optimization_barrier(
                    (have["gelu", c, 0], have["upo", c, 1])
                )
            have[kind, c, k] = plain(
                lambda x, y: jax.nn.gelu(
                    x[:, split[k] * tile : split[k + 1] * tile] + wide(y), approximate=False
                ).astype(jnp.bfloat16),
                have["upw", c],
                have["upo", c, k],
            )
        elif kind in ("do", "dw"):
            first = k + line * (kind == "dw")
            outs = run(
                lambda h, v, after: down_products(h, v, table, first, count, columns, after),
                [have["gelu", c, 0], have["gelu", c, 1]],
                down_weight,
            )
            for i, out in enumerate(outs):
                have["p" + kind[1], c, k + i] = (
                    lax.ppermute(out, "con", swap) if kind == "do" else out
                )
        elif kind == "s":
            out = run(
                lambda h, v, after: stacked_products(h, v, picks[k], line, columns, after),
                [have["gelu", c, 0], have["gelu", c, 1]],
                down_weight,
            )
            have["s" + k, c] = lax.psum_scatter(out, "out", scatter_dimension=0)
        elif kind == "x":
            have[kind, c] = lax.ppermute(have["so", c], "con", swap)
        elif kind == "sum":
            have["fin", c] = plain(
                lambda x, y: (wide(x) + wide(y)).astype(jnp.bfloat16), have["sw", c], have["x", c]
            )
        elif kind == "m":
            out = plain(
                lambda x, y: (wide(x) + wide(y)).astype(jnp.bfloat16),
                have["pw", c, k],
                have["po", c, k],
            )
            have["z", c, k] = lax.ppermute(
                out, "out", [(p, (p + shifts[k]) % line) for p in range(line)]
            )
        else:
            have[kind, c] = plain(
                lambda *terms: sum(wide(term) for term in terms).astype(jnp.bfloat16),
                have["pw", c, line - 1],
                have["po", c, line - 1],
                *[have["z", c, i] for i in range(line - 1)],
            )

    for word in order_of(line):
        task(*word)
    return jnp.concatenate([have["fin", c] for c in range(len(spans))], axis=0)


def solution(mesh):
    in_specs = (
        P("tok", ("con", "out")),
        P(("con", "out")),
        P("con", None, "out"),
        P(("con", "out"), None),
    )
    out_specs = P("tok", ("con", "out"))
    return jax.shard_map(local, mesh=mesh, in_specs=in_specs, out_specs=out_specs, check_vma=False)
```

```python
import functools

import jax
import jax.numpy as jnp
from jax import lax
from jax.experimental import pallas as pl
from jax.experimental.pallas import tpu as pltpu
from jax.sharding import PartitionSpec as P

D = 10240
CHUNKS = (7, 9)
MICROSECOND = 10**6


def order_of(line):
    last = line - 1
    return (
        [("norm", 0), ("upo", 0, 0), ("upo", 0, 1), ("upw", 0), ("gelu", 0, 0), ("gelu", 0, 1)]
        + [("s", 0), ("norm", 1), ("upo", 1, 0), ("upo", 1, 1)]
        + [("upw", 1), ("gelu", 1, 0), ("gelu", 1, 1)]
        + [("do", 1, 0, 1), ("do", 1, 1, 1), ("do", 1, 2, line - 2)]
        + [("dw", 1, 0, 2), ("m", 1, 0), ("dw", 1, 2, 1, 20 * MICROSECOND)]
        + [("m", 1, 1), ("dw", 1, 3, line - 3)]
        + [("m", 1, k) for k in range(2, last)]
        + [("x", 0), ("acc", 1, 0, 0, 60 * MICROSECOND, ("x", 0), ("z", 1, 1))]
        + [("sum", 0), ("fin", 1)]
    )


def tile_of(width):
    return next(tile for tile in (512, 256, 128) if width % tile == 0)


def up_kernel(side_ref, left_ref, right_ref, *refs):
    out_ref = refs[-1]
    out_ref[...] = jnp.dot(
        left_ref[...], right_ref[0], preferred_element_type=jnp.float32
    ).astype(out_ref.dtype)


def up_product(normed, weights, side, first, count, tile, dtype, after):
    rows, depth = normed.shape
    return pl.pallas_call(
        up_kernel,
        grid_spec=pltpu.PrefetchScalarGridSpec(
            num_scalar_prefetch=1,
            grid=(count,),
            in_specs=[
                pl.BlockSpec((rows, depth), lambda j, side: (0, 0)),
                pl.BlockSpec((1, depth, tile), lambda j, side: (side[0], 0, first + j)),
            ]
            + [pl.BlockSpec(memory_space=pl.ANY)] * len(after),
            out_specs=pl.BlockSpec((rows, tile), lambda j, side: (0, j)),
        ),
        out_shape=jax.ShapeDtypeStruct((rows, count * tile), dtype),
        compiler_params=pltpu.CompilerParams(vmem_limit_bytes=40 * 2**20),
        cost_estimate=pl.CostEstimate(flops=1000, bytes_accessed=1000, transcendentals=0),
        name="up_product",
    )(side, normed, weights, *after)


def gelu_kernel(own_ref, other_ref, *refs):
    total = own_ref[...] + other_ref[...].astype(jnp.float32)
    refs[-1][...] = (total * (0.5 + 0.5 * lax.erf(total * 0.5**0.5))).astype(jnp.bfloat16)


def gelu_sum(own, other, first, tile, after):
    rows, width = other.shape
    return pl.pallas_call(
        gelu_kernel,
        grid=(width // tile,),
        in_specs=[
            pl.BlockSpec((rows, tile), lambda j: (0, first + j)),
            pl.BlockSpec((rows, tile), lambda j: (0, j)),
        ]
        + [pl.BlockSpec(memory_space=pl.ANY)] * len(after),
        out_specs=pl.BlockSpec((rows, tile), lambda j: (0, j)),
        out_shape=jax.ShapeDtypeStruct((rows, width), jnp.bfloat16),
        compiler_params=pltpu.CompilerParams(vmem_limit_bytes=40 * 2**20),
        cost_estimate=pl.CostEstimate(flops=1000, bytes_accessed=1000, transcendentals=0),
        name="gelu_sum",
    )(own, other, *after)


def add_kernel(left_ref, right_ref, *refs):
    refs[-1][...] = left_ref[...].astype(jnp.float32) + right_ref[...].astype(jnp.float32)


def add_pieces(left, right, after, weight):
    rows, width = left.shape
    return pl.pallas_call(
        add_kernel,
        grid=(1,),
        in_specs=[pl.BlockSpec((rows, width), lambda j: (0, 0))] * 2
        + [pl.BlockSpec(memory_space=pl.ANY)] * len(after),
        out_specs=pl.BlockSpec((rows, width), lambda j: (0, 0)),
        out_shape=jax.ShapeDtypeStruct((rows, width), jnp.float32),
        compiler_params=pltpu.CompilerParams(vmem_limit_bytes=40 * 2**20),
        cost_estimate=pl.CostEstimate(flops=1000 * weight, bytes_accessed=1000, transcendentals=0),
        name="add_pieces",
    )(left, right, *after)


def down_kernel(parts, waits, blocks_ref, *refs):
    lefts, right_ref, outs = refs[:parts], refs[parts], refs[parts + 1 + waits :]
    total, begin = None, 0
    for left in lefts:
        depth = left.shape[1]
        term = jnp.dot(
            left[...], right_ref[begin : begin + depth, :], preferred_element_type=jnp.float32
        )
        total = term if total is None else total + term
        begin += depth
    for k, out in enumerate(outs):

        @pl.when(pl.program_id(0) == k)
        def _(out=out):
            out[...] = total.astype(out.dtype)


def down_products(hidden, weights, table, first, count, columns, after=(), weight=1):
    rows = hidden[0].shape[0]
    if columns % 128:
        whole = jnp.concatenate(hidden, axis=1)
        return [
            jnp.dot(
                whole,
                lax.dynamic_slice_in_dim(weights, table[first + k] * columns, columns, 1),
                preferred_element_type=jnp.float32,
            ).astype(jnp.bfloat16)
            for k in range(count)
        ]
    return pl.pallas_call(
        functools.partial(down_kernel, len(hidden), len(after)),
        grid_spec=pltpu.PrefetchScalarGridSpec(
            num_scalar_prefetch=1,
            grid=(count,),
            in_specs=[pl.BlockSpec(part.shape, lambda j, table: (0, 0)) for part in hidden]
            + [
                pl.BlockSpec(
                    (weights.shape[0], columns), lambda j, table: (0, table[first + j])
                )
            ]
            + [pl.BlockSpec(memory_space=pl.ANY)] * len(after),
            out_specs=[pl.BlockSpec((rows, columns), lambda j, table: (0, 0))] * count,
        ),
        out_shape=[jax.ShapeDtypeStruct((rows, columns), jnp.bfloat16)] * count,
        compiler_params=pltpu.CompilerParams(vmem_limit_bytes=40 * 2**20),
        cost_estimate=pl.CostEstimate(flops=1000 * weight, bytes_accessed=1000, transcendentals=0),
        name="down_products",
    )(table, *hidden, weights, *after)


def stacked_kernel(parts, side_ref, *refs):
    lefts, right_ref, out_ref = refs[:parts], refs[parts], refs[-1]
    total, begin = None, 0
    for left in lefts:
        depth = left.shape[1]
        term = jnp.dot(
            left[...], right_ref[begin : begin + depth, :], preferred_element_type=jnp.float32
        )
        total = term if total is None else total + term
        begin += depth
    out_ref[0] = total.astype(out_ref.dtype)


def stacked_products(hidden, weights, sides, line, columns, after):
    rows = hidden[0].shape[0]
    if columns % 128:
        both = []
        for s in range(2):
            table = sides[s] * line + jnp.arange(line, dtype=jnp.int32)
            both.append(jnp.stack(down_products(hidden, weights, table, 0, line, columns)))
        return jnp.concatenate(both, axis=2)
    return pl.pallas_call(
        functools.partial(stacked_kernel, len(hidden)),
        grid_spec=pltpu.PrefetchScalarGridSpec(
            num_scalar_prefetch=1,
            grid=(line, 2),
            in_specs=[pl.BlockSpec(piece.shape, lambda p, s, sides: (0, 0)) for piece in hidden]
            + [
                pl.BlockSpec(
                    (weights.shape[0], columns), lambda p, s, sides: (0, sides[s] * line + p)
                )
            ]
            + [pl.BlockSpec(memory_space=pl.ANY)] * len(after),
            out_specs=pl.BlockSpec((1, rows, columns), lambda p, s, sides: (p, 0, s)),
        ),
        out_shape=jax.ShapeDtypeStruct((line, rows, 2 * columns), jnp.bfloat16),
        compiler_params=pltpu.CompilerParams(vmem_limit_bytes=40 * 2**20),
        cost_estimate=pl.CostEstimate(flops=1000, bytes_accessed=1000, transcendentals=0),
        name="stacked_products",
    )(sides, *hidden, weights, *after)


def normalize(values, totals, gain_row):
    average = totals[0][:, None] / D
    variance = totals[1][:, None] / D - average * average
    return ((values - average) * lax.rsqrt(variance + 1e-05) * gain_row).astype(jnp.bfloat16)


def local(tokens, gain, up_weight, down_weight):
    rows, columns = tokens.shape
    line = lax.axis_size("out")
    half, place = lax.axis_index("con"), lax.axis_index("out")
    swap = [(0, 1), (1, 0)]
    wide = lambda x: x.astype(jnp.float32)

    cuts = [rows * sum(CHUNKS[:i]) // sum(CHUNKS) for i in range(len(CHUNKS) + 1)]
    spans = list(zip(cuts[:-1], cuts[1:]))
    gathered = [lax.all_gather(tokens[a:b], "out", axis=1, tiled=True) for a, b in spans]

    values = wide(tokens)
    mine = jnp.stack([jnp.sum(values, axis=1), jnp.sum(values * values, axis=1)])
    shifts = sorted(range(line), key=lambda s: (-min(s, line - s), s))
    row = (place + jnp.array(shifts, jnp.int32)) % line
    table = jnp.concatenate([(1 - half) * line + row, half * line + row])
    here = half.astype(jnp.int32).reshape(1)
    picks = {"o": 1 - here, "w": here, "wo": jnp.concatenate([here, 1 - here])}
    table, picks, mine = lax.optimization_barrier((table, picks, mine))
    mine = mine + lax.ppermute(mine, "con", swap)
    mine = jnp.concatenate([mine.reshape(1, 2 * rows), wide(gain).reshape(1, columns)], axis=1)
    around = [mine] + [
        lax.ppermute(mine, "out", [(p, (p + s) % line) for p in range(line)]) for s in range(1, line)
    ]
    totals = sum(part[0, : 2 * rows] for part in around).reshape(2, rows)
    stacked = jnp.concatenate(around, axis=0)[:, 2 * rows :]
    gain_row = jnp.concatenate(
        [lax.dynamic_index_in_dim(stacked, (place - p + line) % line, 0, False) for p in range(line)]
    )
    totals, gain_row = lax.optimization_barrier((totals, gain_row))

    width = up_weight.shape[2]
    tile = tile_of(width)
    tiles = width // tile
    split = [0, (3 * tiles + 4) // 5, tiles]
    weights = lax.optimization_barrier(jnp.transpose(up_weight, (1, 0, 2)))
    last = [weights]
    have = {}

    def run(f, *args):
        out = f(*args, after=tuple(last))
        last[:] = [out[0] if isinstance(out, (list, tuple)) else out]
        return out

    def plain(f, *args):
        last.append(f(*args))
        return last[-1]

    def task(kind, c, k=0, count=0, weight=1, *awaited):
        last.extend(have[key] for key in awaited)
        a, b = spans[c]
        if kind == "norm":
            have[kind, c] = plain(
                lambda x, t, g: normalize(wide(x), t, g), gathered[c], totals[:, a:b], gain_row
            )
        elif kind == "upo":
            first, count = split[k], split[k + 1] - split[k]
            out = run(
                lambda x, w, after: up_product(
                    x, w, picks["o"], first, count, tile, jnp.bfloat16, after
                ),
                have["norm", c],
                weights,
            )
            have[kind, c, k] = lax.ppermute(out, "con", swap)
        elif kind == "upw":
            have[kind, c] = run(
                lambda x, w, after: up_product(
                    x, w, picks["w"], 0, tiles, tile, jnp.float32, after
                ),
                have["norm", c],
                weights,
            )
        elif kind == "gelu":
            have["gelu", c, k] = run(
                lambda x, y, after: gelu_sum(x, y, split[k], tile, after),
                have["upw", c],
                have["upo", c, k],
            )
        elif kind in ("do", "dw"):
            first = k + line * (kind == "dw")
            outs = run(
                lambda h, v, after: down_products(
                    h, v, table, first, count, columns, after, weight
                ),
                [have["gelu", c, 0], have["gelu", c, 1]],
                down_weight,
            )
            for i, out in enumerate(outs):
                have["p" + kind[1], c, k + i] = (
                    lax.ppermute(out, "con", swap) if kind == "do" else out
                )
        elif kind == "s":
            out = run(
                lambda h, v, after: stacked_products(h, v, picks["wo"], line, columns, after),
                [have["gelu", c, 0], have["gelu", c, 1]],
                down_weight,
            )
            have[kind, c] = lax.psum_scatter(out, "out", scatter_dimension=0)
        elif kind == "x":
            have[kind, c] = lax.ppermute(have["s", c][:, columns:], "con", swap)
        elif kind == "sum":
            have["fin", c] = plain(
                lambda x, y: (wide(x[:, :columns]) + wide(y)).astype(jnp.bfloat16),
                have["s", c],
                have["x", c],
            )
        elif kind == "m":
            out = plain(
                lambda x, y: (wide(x) + wide(y)).astype(jnp.bfloat16),
                have["pw", c, k],
                have["po", c, k],
            )
            have["z", c, k] = lax.ppermute(
                out, "out", [(p, (p + shifts[k]) % line) for p in range(line)]
            )
        elif kind == "acc":
            have[kind, c] = run(
                lambda x, y, after: add_pieces(x, y, after, weight),
                have["pw", c, line - 1],
                have["z", c, 0],
            )
        else:
            have[kind, c] = plain(
                lambda *terms: sum(wide(term) for term in terms).astype(jnp.bfloat16),
                have["acc", c],
                have["po", c, line - 1],
                *[have["z", c, i] for i in range(1, line - 1)],
            )

    for word in order_of(line):
        task(*word)
    return jnp.concatenate([have["fin", c] for c in range(len(spans))], axis=0)


def solution(mesh):
    in_specs = (
        P("tok", ("con", "out")),
        P(("con", "out")),
        P("con", None, "out"),
        P(("con", "out"), None),
    )
    out_specs = P("tok", ("con", "out"))
    return jax.shard_map(local, mesh=mesh, in_specs=in_specs, out_specs=out_specs, check_vma=False)
```

```python
import functools

import jax
import jax.numpy as jnp
from jax import lax
from jax.experimental import pallas as pl
from jax.experimental.pallas import tpu as pltpu
from jax.sharding import PartitionSpec as P

D = 10240
CHUNKS = (7, 9)
MICROSECOND = 10**6


def order_of(line):
    last = line - 1
    return (
        [("norm", 0), ("upo", 0, 0), ("upo", 0, 1), ("upw", 0), ("gelu", 0, 0), ("gelu", 0, 1)]
        + [("s", 0), ("norm", 1), ("upo", 1, 0), ("upo", 1, 1)]
        + [("upw", 1), ("gelu", 1, 0), ("gelu", 1, 1)]
        + [("do", 1, 0, 1), ("dw", 1, 0, 1), ("do", 1, 1, 1), ("do", 1, 2, line - 2), ("m", 1, 0)]
        + [("dw", 1, 1, 1, 20 * MICROSECOND), ("m", 1, 1), ("dw", 1, 2, line - 2)]
        + [("m", 1, k) for k in range(2, last)]
        + [("x", 0), ("acc", 1, 0, 0, 60 * MICROSECOND, ("x", 0), ("z", 1, 1))]
        + [("sum", 0), ("fin", 1)]
    )


def tile_of(width):
    return next(tile for tile in (512, 256, 128) if width % tile == 0)


def up_kernel(side_ref, left_ref, right_ref, *refs):
    out_ref = refs[-1]
    out_ref[...] = jnp.dot(
        left_ref[...], right_ref[0], preferred_element_type=jnp.float32
    ).astype(out_ref.dtype)


def up_product(normed, weights, side, first, count, tile, dtype, after):
    rows, depth = normed.shape
    return pl.pallas_call(
        up_kernel,
        grid_spec=pltpu.PrefetchScalarGridSpec(
            num_scalar_prefetch=1,
            grid=(count,),
            in_specs=[
                pl.BlockSpec((rows, depth), lambda j, side: (0, 0)),
                pl.BlockSpec((1, depth, tile), lambda j, side: (side[0], 0, first + j)),
            ]
            + [pl.BlockSpec(memory_space=pl.ANY)] * len(after),
            out_specs=pl.BlockSpec((rows, tile), lambda j, side: (0, j)),
        ),
        out_shape=jax.ShapeDtypeStruct((rows, count * tile), dtype),
        compiler_params=pltpu.CompilerParams(vmem_limit_bytes=40 * 2**20),
        cost_estimate=pl.CostEstimate(flops=1000, bytes_accessed=1000, transcendentals=0),
        name="up_product",
    )(side, normed, weights, *after)


def gelu_kernel(own_ref, other_ref, *refs):
    total = own_ref[...] + other_ref[...].astype(jnp.float32)
    refs[-1][...] = (total * (0.5 + 0.5 * lax.erf(total * 0.5**0.5))).astype(jnp.bfloat16)


def gelu_sum(own, other, first, tile, after):
    rows, width = other.shape
    return pl.pallas_call(
        gelu_kernel,
        grid=(width // tile,),
        in_specs=[
            pl.BlockSpec((rows, tile), lambda j: (0, first + j)),
            pl.BlockSpec((rows, tile), lambda j: (0, j)),
        ]
        + [pl.BlockSpec(memory_space=pl.ANY)] * len(after),
        out_specs=pl.BlockSpec((rows, tile), lambda j: (0, j)),
        out_shape=jax.ShapeDtypeStruct((rows, width), jnp.bfloat16),
        compiler_params=pltpu.CompilerParams(vmem_limit_bytes=40 * 2**20),
        cost_estimate=pl.CostEstimate(flops=1000, bytes_accessed=1000, transcendentals=0),
        name="gelu_sum",
    )(own, other, *after)


def add_kernel(left_ref, right_ref, *refs):
    refs[-1][...] = left_ref[...].astype(jnp.float32) + right_ref[...].astype(jnp.float32)


def add_pieces(left, right, after, weight):
    rows, width = left.shape
    return pl.pallas_call(
        add_kernel,
        grid=(1,),
        in_specs=[pl.BlockSpec((rows, width), lambda j: (0, 0))] * 2
        + [pl.BlockSpec(memory_space=pl.ANY)] * len(after),
        out_specs=pl.BlockSpec((rows, width), lambda j: (0, 0)),
        out_shape=jax.ShapeDtypeStruct((rows, width), jnp.float32),
        compiler_params=pltpu.CompilerParams(vmem_limit_bytes=40 * 2**20),
        cost_estimate=pl.CostEstimate(flops=1000 * weight, bytes_accessed=1000, transcendentals=0),
        name="add_pieces",
    )(left, right, *after)


def down_kernel(parts, waits, blocks_ref, *refs):
    lefts, right_ref, outs = refs[:parts], refs[parts], refs[parts + 1 + waits :]
    total, begin = None, 0
    for left in lefts:
        depth = left.shape[1]
        term = jnp.dot(
            left[...], right_ref[begin : begin + depth, :], preferred_element_type=jnp.float32
        )
        total = term if total is None else total + term
        begin += depth
    for k, out in enumerate(outs):

        @pl.when(pl.program_id(0) == k)
        def _(out=out):
            out[...] = total.astype(out.dtype)


def down_products(hidden, weights, table, first, count, columns, after=(), weight=1):
    rows = hidden[0].shape[0]
    if columns % 128:
        whole = jnp.concatenate(hidden, axis=1)
        return [
            jnp.dot(
                whole,
                lax.dynamic_slice_in_dim(weights, table[first + k] * columns, columns, 1),
                preferred_element_type=jnp.float32,
            ).astype(jnp.bfloat16)
            for k in range(count)
        ]
    return pl.pallas_call(
        functools.partial(down_kernel, len(hidden), len(after)),
        grid_spec=pltpu.PrefetchScalarGridSpec(
            num_scalar_prefetch=1,
            grid=(count,),
            in_specs=[pl.BlockSpec(part.shape, lambda j, table: (0, 0)) for part in hidden]
            + [
                pl.BlockSpec(
                    (weights.shape[0], columns), lambda j, table: (0, table[first + j])
                )
            ]
            + [pl.BlockSpec(memory_space=pl.ANY)] * len(after),
            out_specs=[pl.BlockSpec((rows, columns), lambda j, table: (0, 0))] * count,
        ),
        out_shape=[jax.ShapeDtypeStruct((rows, columns), jnp.bfloat16)] * count,
        compiler_params=pltpu.CompilerParams(vmem_limit_bytes=40 * 2**20),
        cost_estimate=pl.CostEstimate(flops=1000 * weight, bytes_accessed=1000, transcendentals=0),
        name="down_products",
    )(table, *hidden, weights, *after)


def stacked_kernel(parts, side_ref, *refs):
    lefts, right_ref, out_ref = refs[:parts], refs[parts], refs[-1]
    total, begin = None, 0
    for left in lefts:
        depth = left.shape[1]
        term = jnp.dot(
            left[...], right_ref[begin : begin + depth, :], preferred_element_type=jnp.float32
        )
        total = term if total is None else total + term
        begin += depth
    out_ref[0] = total.astype(out_ref.dtype)


def stacked_products(hidden, weights, sides, line, columns, after):
    rows = hidden[0].shape[0]
    if columns % 128:
        both = []
        for s in range(2):
            table = sides[s] * line + jnp.arange(line, dtype=jnp.int32)
            both.append(jnp.stack(down_products(hidden, weights, table, 0, line, columns)))
        return jnp.concatenate(both, axis=2)
    return pl.pallas_call(
        functools.partial(stacked_kernel, len(hidden)),
        grid_spec=pltpu.PrefetchScalarGridSpec(
            num_scalar_prefetch=1,
            grid=(line, 2),
            in_specs=[pl.BlockSpec(piece.shape, lambda p, s, sides: (0, 0)) for piece in hidden]
            + [
                pl.BlockSpec(
                    (weights.shape[0], columns), lambda p, s, sides: (0, sides[s] * line + p)
                )
            ]
            + [pl.BlockSpec(memory_space=pl.ANY)] * len(after),
            out_specs=pl.BlockSpec((1, rows, columns), lambda p, s, sides: (p, 0, s)),
        ),
        out_shape=jax.ShapeDtypeStruct((line, rows, 2 * columns), jnp.bfloat16),
        compiler_params=pltpu.CompilerParams(vmem_limit_bytes=40 * 2**20),
        cost_estimate=pl.CostEstimate(flops=1000, bytes_accessed=1000, transcendentals=0),
        name="stacked_products",
    )(sides, *hidden, weights, *after)


def normalize(values, totals, gain_row):
    average = totals[0][:, None] / D
    variance = totals[1][:, None] / D - average * average
    return ((values - average) * lax.rsqrt(variance + 1e-05) * gain_row).astype(jnp.bfloat16)


def local(tokens, gain, up_weight, down_weight):
    rows, columns = tokens.shape
    line = lax.axis_size("out")
    half, place = lax.axis_index("con"), lax.axis_index("out")
    swap = [(0, 1), (1, 0)]
    wide = lambda x: x.astype(jnp.float32)

    cuts = [rows * sum(CHUNKS[:i]) // sum(CHUNKS) for i in range(len(CHUNKS) + 1)]
    spans = list(zip(cuts[:-1], cuts[1:]))
    gathered = [lax.all_gather(tokens[a:b], "out", axis=1, tiled=True) for a, b in spans]

    values = wide(tokens)
    mine = jnp.stack([jnp.sum(values, axis=1), jnp.sum(values * values, axis=1)])
    four = line == 4
    if four:
        shifts = [3, 1, 2, 0]
        row = jnp.stack([place ^ s for s in shifts])
    else:
        shifts = sorted(range(line), key=lambda s: (-min(s, line - s), s))
        row = (place + jnp.array(shifts, jnp.int32)) % line
    table = jnp.concatenate([(1 - half) * line + row, half * line + row])
    here = half.astype(jnp.int32).reshape(1)
    picks = {"o": 1 - here, "w": here, "wo": jnp.concatenate([here, 1 - here])}
    table, picks, mine = lax.optimization_barrier((table, picks, mine))
    mine = mine + lax.ppermute(mine, "con", swap)
    mine = jnp.concatenate([mine.reshape(1, 2 * rows), wide(gain).reshape(1, columns)], axis=1)
    around = [mine] + [
        lax.ppermute(mine, "out", [(p, (p + s) % line) for p in range(line)]) for s in range(1, line)
    ]
    totals = sum(part[0, : 2 * rows] for part in around).reshape(2, rows)
    stacked = jnp.concatenate(around, axis=0)[:, 2 * rows :]
    gain_row = jnp.concatenate(
        [lax.dynamic_index_in_dim(stacked, (place - p + line) % line, 0, False) for p in range(line)]
    )
    totals, gain_row = lax.optimization_barrier((totals, gain_row))

    width = up_weight.shape[2]
    tile = tile_of(width)
    tiles = width // tile
    split = [0, (3 * tiles + 4) // 5, tiles]
    weights = lax.optimization_barrier(jnp.transpose(up_weight, (1, 0, 2)))
    last = [weights]
    have = {}

    def run(f, *args):
        out = f(*args, after=tuple(last))
        last[:] = [out[0] if isinstance(out, (list, tuple)) else out]
        return out

    def plain(f, *args):
        last.append(f(*args))
        return last[-1]

    def task(kind, c, k=0, count=0, weight=1, *awaited):
        last.extend(have[key] for key in awaited)
        a, b = spans[c]
        if kind == "norm":
            have[kind, c] = plain(
                lambda x, t, g: normalize(wide(x), t, g), gathered[c], totals[:, a:b], gain_row
            )
        elif kind == "upo":
            first, count = split[k], split[k + 1] - split[k]
            out = run(
                lambda x, w, after: up_product(
                    x, w, picks["o"], first, count, tile, jnp.bfloat16, after
                ),
                have["norm", c],
                weights,
            )
            have[kind, c, k] = lax.ppermute(out, "con", swap)
        elif kind == "upw":
            have[kind, c] = run(
                lambda x, w, after: up_product(
                    x, w, picks["w"], 0, tiles, tile, jnp.float32, after
                ),
                have["norm", c],
                weights,
            )
        elif kind == "gelu":
            have["gelu", c, k] = run(
                lambda x, y, after: gelu_sum(x, y, split[k], tile, after),
                have["upw", c],
                have["upo", c, k],
            )
        elif kind in ("do", "dw"):
            first = k + line * (kind == "dw")
            outs = run(
                lambda h, v, after: down_products(
                    h, v, table, first, count, columns, after, weight
                ),
                [have["gelu", c, 0], have["gelu", c, 1]],
                down_weight,
            )
            for i, out in enumerate(outs):
                have["p" + kind[1], c, k + i] = (
                    lax.ppermute(out, "con", swap) if kind == "do" else out
                )
        elif kind == "s":
            out = run(
                lambda h, v, after: stacked_products(h, v, picks["wo"], line, columns, after),
                [have["gelu", c, 0], have["gelu", c, 1]],
                down_weight,
            )
            have[kind, c] = lax.psum_scatter(out, "out", scatter_dimension=0)
        elif kind == "x":
            have[kind, c] = lax.ppermute(have["s", c][:, columns:], "con", swap)
        elif kind == "sum":
            have["fin", c] = plain(
                lambda x, y: (wide(x[:, :columns]) + wide(y)).astype(jnp.bfloat16),
                have["s", c],
                have["x", c],
            )
        elif kind == "m":
            terms = [have["pw", c, k], have["po", c, k]]
            if four and k == 2:
                terms.append(have["ends", c])
            out = plain(lambda *terms: sum(map(wide, terms)).astype(jnp.bfloat16), *terms)
            if four and k == 0:
                have["ends", c] = lax.ppermute(out, "out", [(0, 1), (3, 2)])
                pairs = [(1, 2), (2, 1)]
            elif four:
                pairs = [(p, p ^ shifts[k]) for p in range(line)]
            else:
                pairs = [(p, (p + shifts[k]) % line) for p in range(line)]
            have["z", c, k] = lax.ppermute(out, "out", pairs)
        elif kind == "acc":
            have[kind, c] = run(
                lambda x, y, after: add_pieces(x, y, after, weight),
                have["pw", c, line - 1],
                have["z", c, 0],
            )
        else:
            have[kind, c] = plain(
                lambda *terms: sum(wide(term) for term in terms).astype(jnp.bfloat16),
                have["acc", c],
                have["po", c, line - 1],
                *[have["z", c, i] for i in range(1, line - 1)],
            )

    for word in order_of(line):
        task(*word)
    return jnp.concatenate([have["fin", c] for c in range(len(spans))], axis=0)


def solution(mesh):
    in_specs = (
        P("tok", ("con", "out")),
        P(("con", "out")),
        P("con", None, "out"),
        P(("con", "out"), None),
    )
    out_specs = P("tok", ("con", "out"))
    return jax.shard_map(local, mesh=mesh, in_specs=in_specs, out_specs=out_specs, check_vma=False)
```

```python
import functools

import jax
import jax.numpy as jnp
from jax import lax
from jax.experimental import pallas as pl
from jax.experimental.pallas import tpu as pltpu
from jax.sharding import PartitionSpec as P

D = 10240
CHUNKS = (7, 9)
MICROSECOND = 10**6


def order_of(line):
    last = line - 1
    return (
        [("norm", 0), ("upo", 0, 0), ("upo", 0, 1), ("upw", 0), ("gelu", 0, 0), ("gelu", 0, 1)]
        + [("s", 0), ("norm", 1), ("upo", 1, 0), ("upo", 1, 1)]
        + [("upw", 1), ("gelu", 1, 0), ("gelu", 1, 1)]
        + [("do", 1, 0, 1), ("dw", 1, 0, 1), ("do", 1, 1, 1), ("do", 1, 2, line - 2), ("m", 1, 0)]
        + [("dw", 1, 1, 1, 20 * MICROSECOND), ("m", 1, 1), ("dw", 1, 2, line - 2)]
        + [("m", 1, k) for k in range(2, last)]
        + [("x", 0), ("acc", 1, 0, 0, 60 * MICROSECOND, ("x", 0), ("z", 1, 1))]
        + [("sum", 0), ("fin", 1)]
    )


def tile_of(width):
    return next(tile for tile in (512, 256, 128) if width % tile == 0)


def up_kernel(side_ref, left_ref, right_ref, *refs):
    out_ref = refs[-1]
    out_ref[...] = jnp.dot(
        left_ref[...], right_ref[0], preferred_element_type=jnp.float32
    ).astype(out_ref.dtype)


def up_product(normed, weights, side, first, count, tile, dtype, after):
    rows, depth = normed.shape
    return pl.pallas_call(
        up_kernel,
        grid_spec=pltpu.PrefetchScalarGridSpec(
            num_scalar_prefetch=1,
            grid=(count,),
            in_specs=[
                pl.BlockSpec((rows, depth), lambda j, side: (0, 0)),
                pl.BlockSpec((1, depth, tile), lambda j, side: (side[0], 0, first + j)),
            ]
            + [pl.BlockSpec(memory_space=pl.ANY)] * len(after),
            out_specs=pl.BlockSpec((rows, tile), lambda j, side: (0, j)),
        ),
        out_shape=jax.ShapeDtypeStruct((rows, count * tile), dtype),
        compiler_params=pltpu.CompilerParams(vmem_limit_bytes=40 * 2**20),
        cost_estimate=pl.CostEstimate(flops=1000, bytes_accessed=1000, transcendentals=0),
        name="up_product",
    )(side, normed, weights, *after)


def gelu_kernel(own_ref, other_ref, *refs):
    total = own_ref[...] + other_ref[...].astype(jnp.float32)
    refs[-1][...] = (total * (0.5 + 0.5 * lax.erf(total * 0.5**0.5))).astype(jnp.bfloat16)


def gelu_sum(own, other, first, tile, after):
    rows, width = other.shape
    return pl.pallas_call(
        gelu_kernel,
        grid=(width // tile,),
        in_specs=[
            pl.BlockSpec((rows, tile), lambda j: (0, first + j)),
            pl.BlockSpec((rows, tile), lambda j: (0, j)),
        ]
        + [pl.BlockSpec(memory_space=pl.ANY)] * len(after),
        out_specs=pl.BlockSpec((rows, tile), lambda j: (0, j)),
        out_shape=jax.ShapeDtypeStruct((rows, width), jnp.bfloat16),
        compiler_params=pltpu.CompilerParams(vmem_limit_bytes=40 * 2**20),
        cost_estimate=pl.CostEstimate(flops=1000, bytes_accessed=1000, transcendentals=0),
        name="gelu_sum",
    )(own, other, *after)


def add_kernel(left_ref, right_ref, *refs):
    refs[-1][...] = left_ref[...].astype(jnp.float32) + right_ref[...].astype(jnp.float32)


def add_pieces(left, right, after, weight):
    rows, width = left.shape
    return pl.pallas_call(
        add_kernel,
        grid=(1,),
        in_specs=[pl.BlockSpec((rows, width), lambda j: (0, 0))] * 2
        + [pl.BlockSpec(memory_space=pl.ANY)] * len(after),
        out_specs=pl.BlockSpec((rows, width), lambda j: (0, 0)),
        out_shape=jax.ShapeDtypeStruct((rows, width), jnp.float32),
        compiler_params=pltpu.CompilerParams(vmem_limit_bytes=40 * 2**20),
        cost_estimate=pl.CostEstimate(flops=1000 * weight, bytes_accessed=1000, transcendentals=0),
        name="add_pieces",
    )(left, right, *after)


def finish_kernel(first_ref, *refs):
    terms, out_ref = refs[:-1], refs[-1]
    rows = first_ref.shape[0]
    out_ref[:rows, :] = first_ref[...]
    total = terms[0][...]
    for term in terms[1:]:
        total = total + term[...].astype(jnp.float32)
    out_ref[rows:, :] = total.astype(out_ref.dtype)


def finish(first, *terms):
    rows = first.shape[0] + terms[0].shape[0]
    return pl.pallas_call(
        finish_kernel,
        out_shape=jax.ShapeDtypeStruct((rows, first.shape[1]), jnp.bfloat16),
        compiler_params=pltpu.CompilerParams(vmem_limit_bytes=40 * 2**20),
        cost_estimate=pl.CostEstimate(flops=1000, bytes_accessed=1000, transcendentals=0),
        name="finish",
    )(first, *terms)


def down_kernel(parts, waits, blocks_ref, *refs):
    lefts, right_ref, outs = refs[:parts], refs[parts], refs[parts + 1 + waits :]
    total, begin = None, 0
    for left in lefts:
        depth = left.shape[1]
        term = jnp.dot(
            left[...], right_ref[begin : begin + depth, :], preferred_element_type=jnp.float32
        )
        total = term if total is None else total + term
        begin += depth
    for k, out in enumerate(outs):

        @pl.when(pl.program_id(0) == k)
        def _(out=out):
            out[...] = total.astype(out.dtype)


def down_products(hidden, weights, table, first, count, columns, after=(), weight=1):
    rows = hidden[0].shape[0]
    if columns % 128:
        whole = jnp.concatenate(hidden, axis=1)
        return [
            jnp.dot(
                whole,
                lax.dynamic_slice_in_dim(weights, table[first + k] * columns, columns, 1),
                preferred_element_type=jnp.float32,
            ).astype(jnp.bfloat16)
            for k in range(count)
        ]
    return pl.pallas_call(
        functools.partial(down_kernel, len(hidden), len(after)),
        grid_spec=pltpu.PrefetchScalarGridSpec(
            num_scalar_prefetch=1,
            grid=(count,),
            in_specs=[pl.BlockSpec(part.shape, lambda j, table: (0, 0)) for part in hidden]
            + [
                pl.BlockSpec(
                    (weights.shape[0], columns), lambda j, table: (0, table[first + j])
                )
            ]
            + [pl.BlockSpec(memory_space=pl.ANY)] * len(after),
            out_specs=[pl.BlockSpec((rows, columns), lambda j, table: (0, 0))] * count,
        ),
        out_shape=[jax.ShapeDtypeStruct((rows, columns), jnp.bfloat16)] * count,
        compiler_params=pltpu.CompilerParams(vmem_limit_bytes=40 * 2**20),
        cost_estimate=pl.CostEstimate(flops=1000 * weight, bytes_accessed=1000, transcendentals=0),
        name="down_products",
    )(table, *hidden, weights, *after)


def stacked_kernel(parts, side_ref, *refs):
    lefts, right_ref, out_ref = refs[:parts], refs[parts], refs[-1]
    total, begin = None, 0
    for left in lefts:
        depth = left.shape[1]
        term = jnp.dot(
            left[...], right_ref[begin : begin + depth, :], preferred_element_type=jnp.float32
        )
        total = term if total is None else total + term
        begin += depth
    out_ref[0] = total.astype(out_ref.dtype)


def stacked_products(hidden, weights, sides, line, columns, after):
    rows = hidden[0].shape[0]
    if columns % 128:
        both = []
        for s in range(2):
            table = sides[s] * line + jnp.arange(line, dtype=jnp.int32)
            both.append(jnp.stack(down_products(hidden, weights, table, 0, line, columns)))
        return jnp.concatenate(both, axis=2)
    return pl.pallas_call(
        functools.partial(stacked_kernel, len(hidden)),
        grid_spec=pltpu.PrefetchScalarGridSpec(
            num_scalar_prefetch=1,
            grid=(line, 2),
            in_specs=[pl.BlockSpec(piece.shape, lambda p, s, sides: (0, 0)) for piece in hidden]
            + [
                pl.BlockSpec(
                    (weights.shape[0], columns), lambda p, s, sides: (0, sides[s] * line + p)
                )
            ]
            + [pl.BlockSpec(memory_space=pl.ANY)] * len(after),
            out_specs=pl.BlockSpec((1, rows, columns), lambda p, s, sides: (p, 0, s)),
        ),
        out_shape=jax.ShapeDtypeStruct((line, rows, 2 * columns), jnp.bfloat16),
        compiler_params=pltpu.CompilerParams(vmem_limit_bytes=40 * 2**20),
        cost_estimate=pl.CostEstimate(flops=1000, bytes_accessed=1000, transcendentals=0),
        name="stacked_products",
    )(sides, *hidden, weights, *after)


def normalize(values, totals, gain_row):
    average = totals[0][:, None] / D
    variance = totals[1][:, None] / D - average * average
    return ((values - average) * lax.rsqrt(variance + 1e-05) * gain_row).astype(jnp.bfloat16)


def local(tokens, gain, up_weight, down_weight):
    rows, columns = tokens.shape
    line = lax.axis_size("out")
    half, place = lax.axis_index("con"), lax.axis_index("out")
    swap = [(0, 1), (1, 0)]
    wide = lambda x: x.astype(jnp.float32)

    cuts = [rows * sum(CHUNKS[:i]) // sum(CHUNKS) for i in range(len(CHUNKS) + 1)]
    spans = list(zip(cuts[:-1], cuts[1:]))
    gathered = [lax.all_gather(tokens[a:b], "out", axis=1, tiled=True) for a, b in spans]

    values = wide(tokens)
    mine = jnp.stack([jnp.sum(values, axis=1), jnp.sum(values * values, axis=1)])
    four = line == 4
    if four:
        shifts = [3, 1, 2, 0]
        row = jnp.stack([place ^ s for s in shifts])
    else:
        shifts = sorted(range(line), key=lambda s: (-min(s, line - s), s))
        row = (place + jnp.array(shifts, jnp.int32)) % line
    table = jnp.concatenate([(1 - half) * line + row, half * line + row])
    here = half.astype(jnp.int32).reshape(1)
    picks = {"o": 1 - here, "w": here, "wo": jnp.concatenate([here, 1 - here])}
    table, picks, mine = lax.optimization_barrier((table, picks, mine))
    mine = mine + lax.ppermute(mine, "con", swap)
    mine = jnp.concatenate([mine.reshape(1, 2 * rows), wide(gain).reshape(1, columns)], axis=1)
    around = [mine] + [
        lax.ppermute(mine, "out", [(p, (p + s) % line) for p in range(line)]) for s in range(1, line)
    ]
    totals = sum(part[0, : 2 * rows] for part in around).reshape(2, rows)
    stacked = jnp.concatenate(around, axis=0)[:, 2 * rows :]
    gain_row = jnp.concatenate(
        [lax.dynamic_index_in_dim(stacked, (place - p + line) % line, 0, False) for p in range(line)]
    )
    totals, gain_row = lax.optimization_barrier((totals, gain_row))

    width = up_weight.shape[2]
    tile = tile_of(width)
    tiles = width // tile
    split = [0, (3 * tiles + 4) // 5, tiles]
    weights = lax.optimization_barrier(jnp.transpose(up_weight, (1, 0, 2)))
    last = [weights]
    have = {}

    def run(f, *args):
        out = f(*args, after=tuple(last))
        last[:] = [out[0] if isinstance(out, (list, tuple)) else out]
        return out

    def plain(f, *args):
        last.append(f(*args))
        return last[-1]

    def task(kind, c, k=0, count=0, weight=1, *awaited):
        last.extend(have[key] for key in awaited)
        a, b = spans[c]
        if kind == "norm":
            have[kind, c] = plain(
                lambda x, t, g: normalize(wide(x), t, g), gathered[c], totals[:, a:b], gain_row
            )
        elif kind == "upo":
            first, count = split[k], split[k + 1] - split[k]
            out = run(
                lambda x, w, after: up_product(
                    x, w, picks["o"], first, count, tile, jnp.bfloat16, after
                ),
                have["norm", c],
                weights,
            )
            have[kind, c, k] = lax.ppermute(out, "con", swap)
        elif kind == "upw":
            have[kind, c] = run(
                lambda x, w, after: up_product(
                    x, w, picks["w"], 0, tiles, tile, jnp.float32, after
                ),
                have["norm", c],
                weights,
            )
        elif kind == "gelu":
            have["gelu", c, k] = run(
                lambda x, y, after: gelu_sum(x, y, split[k], tile, after),
                have["upw", c],
                have["upo", c, k],
            )
        elif kind in ("do", "dw"):
            first = k + line * (kind == "dw")
            outs = run(
                lambda h, v, after: down_products(
                    h, v, table, first, count, columns, after, weight
                ),
                [have["gelu", c, 0], have["gelu", c, 1]],
                down_weight,
            )
            for i, out in enumerate(outs):
                have["p" + kind[1], c, k + i] = (
                    lax.ppermute(out, "con", swap) if kind == "do" else out
                )
        elif kind == "s":
            out = run(
                lambda h, v, after: stacked_products(h, v, picks["wo"], line, columns, after),
                [have["gelu", c, 0], have["gelu", c, 1]],
                down_weight,
            )
            have[kind, c] = lax.psum_scatter(out, "out", scatter_dimension=0)
        elif kind == "x":
            have[kind, c] = lax.ppermute(have["s", c][:, columns:], "con", swap)
        elif kind == "sum":
            have["fin", c] = plain(
                lambda x, y: (wide(x[:, :columns]) + wide(y)).astype(jnp.bfloat16),
                have["s", c],
                have["x", c],
            )
        elif kind == "m":
            terms = [have["pw", c, k], have["po", c, k]]
            if four and k == 2:
                terms.append(have["ends", c])
            out = plain(lambda *terms: sum(map(wide, terms)).astype(jnp.bfloat16), *terms)
            if k == line - 2:
                out, have["s", 0] = lax.optimization_barrier((out, have["s", 0]))
            if four and k == 0:
                have["ends", c] = lax.ppermute(out, "out", [(0, 1), (3, 2)])
                pairs = [(1, 2), (2, 1)]
            elif four:
                pairs = [(p, p ^ shifts[k]) for p in range(line)]
            else:
                pairs = [(p, (p + shifts[k]) % line) for p in range(line)]
            have["z", c, k] = lax.ppermute(out, "out", pairs)
        elif kind == "acc":
            have[kind, c] = run(
                lambda x, y, after: add_pieces(x, y, after, weight),
                have["pw", c, line - 1],
                have["z", c, 0],
            )
        else:
            have[kind, c] = finish(
                have["fin", 0],
                have["acc", c],
                have["po", c, line - 1],
                *[have["z", c, i] for i in range(1, line - 1)],
            )

    for word in order_of(line):
        task(*word)
    return have["fin", 1]


def solution(mesh):
    in_specs = (
        P("tok", ("con", "out")),
        P(("con", "out")),
        P("con", None, "out"),
        P(("con", "out"), None),
    )
    out_specs = P("tok", ("con", "out"))
    return jax.shard_map(local, mesh=mesh, in_specs=in_specs, out_specs=out_specs, check_vma=False)
```
